512 devices in a mesh: layer: 8 (over y), row: 16 (over z, core), col: 4 (over x).
Axes of the slice: x: 4, y: 8, z: 8, core: 2. Of those that a mesh axis runs over, the one named last changes fastest.
Arguments:
- front_inv: float32 [8, 6144, 4, 1536], P('layer', 'row', 'col'), may hold values from -0.078125 to 0.078125
- impedance: float32 [8, 6144], P('layer', ('row', 'col')), may hold values from 0.3 to 1
- sources: float32 [8, 3, 4, 1536, 128], P('layer', None, 'col'), may hold values from -6 to 6
Outputs:
- outgoing: float32 [8, 3, 6144, 128], P('layer', None, ('row', 'col'))
The draws below stay inside these ranges and needn't reach their ends.
All inputs are finite; a program needn't handle non-finite values.
Results may differ from the reference program's by a relative error of at most 0.0001.
Values sent between devices are 32-bit elements; how exact they have to be, the bound alone decides.
A program may use at most 64 MiB of HBM per device.

```python
import math
import jax
import jax.numpy as jnp
from jax import lax

F = 6144
B = 128
NB = 3
FRONTS = 8
E = 96
N_ROW = 16
N_COL = 4


def block_levels(rng, dims, cuts, smallest, largest):
    gain = 1.0
    for axis_at, shards_of in cuts:
        steps = jax.random.uniform(jax.random.fold_in(jax.random.fold_in(rng, 6), axis_at), (shards_of,), jnp.float32, smallest / len(cuts), largest / len(cuts))
        gain = gain * jnp.repeat(jnp.exp(steps), dims[axis_at] // shards_of).reshape((-1,) + (1,) * (len(dims) - 1 - axis_at))
    return gain


def normal_values(own_key, extent, spread, bound, pieces=(), held_as=jnp.bfloat16):
    factor_of = block_levels(own_key, extent, pieces, -0.22, 0.18) if pieces else 1.0
    drawn = jax.random.normal(own_key, extent, jnp.float32) * spread * factor_of
    return jnp.minimum(jnp.maximum(drawn, -bound), bound).astype(held_as)


def setup_inputs(seed: int = 0) -> dict:
    key_list = jax.random.split(jax.random.key(seed), 4)
    return {
        "front_inv": normal_values(key_list[0], (FRONTS, F, N_COL, F // N_COL), F ** -0.5, 0.078125, ((0, 8), (1, 16), (2, 4)), jnp.float32),
        "impedance": jnp.clip(jnp.exp(math.log(1.0) - 1.2039728 * jax.random.uniform(key_list[1], (FRONTS, F), jnp.float32) ** block_levels(key_list[1], (FRONTS, F), ((0, 8), (1, 64)), -0.2, 0.2)), 0.3, 1.0),
        "sources": normal_values(key_list[2], (FRONTS, NB, N_COL, F // N_COL, B), 1.0, 6.0, ((0, 8), (2, 4)), jnp.float32),
    }


def reference(front_inv, impedance, sources):
    matrix_all = front_inv.reshape(FRONTS, F, N_COL, N_ROW, E).transpose(0, 1, 3, 2, 4).reshape(FRONTS, F, F)
    own_all = sources.reshape(FRONTS, NB, N_COL, N_ROW, E, B).transpose(0, 1, 3, 2, 4, 5).reshape(FRONTS, NB, F, B)
    results = []
    carried = None
    for layer_id in range(FRONTS):
        outputs = []
        for block_id in range(NB):
            current = own_all[layer_id, block_id]
            if carried is not None:
                current = current + carried[block_id]
            product = jnp.dot(matrix_all[layer_id], current, precision=lax.Precision.HIGHEST, preferred_element_type=jnp.float32)
            outputs.append(impedance[layer_id][:, None] * product)
        carried = outputs
        results.append(jnp.stack(outputs))
    return jnp.stack(results)
```

```python
import functools

import jax
import jax.numpy as jnp
from jax import lax
from jax.experimental import pallas as pl
from jax.experimental.pallas import tpu as pltpu
from jax.sharding import PartitionSpec as P

MESH = pl.DeviceIdType.MESH
F32, BF16 = jnp.float32, jnp.bfloat16
LANES = 128
GROUPS = 4
WIDE = LANES // GROUPS
LAG = 2


def pick(parts):
    group = lax.broadcasted_iota(jnp.int32, parts[0].shape, 1) // WIDE
    result = parts[0]
    for g in range(1, GROUPS):
        result = jnp.where(group == g, parts[g], result)
    return result


def turned(x, by):
    by = by % GROUPS
    return x if by == 0 else pltpu.roll(x, by * WIDE, 1)


def swapped(parts):
    return [pick([turned(parts[a], a - b) for a in range(GROUPS)]) for b in range(GROUPS)]


def sweep(sizes, front, impedance, sources, out, m_own, m_other, m_parts, src, own, ag_in, vec, rs_out, rs_in, ag_out,
          from_other, scale, load_sem, swap_send, swap_recv, rs_send, rs_recv, ag_send, ag_recv, out_send, out_recv):
    layers, chips, cols = sizes
    layer, row, col = lax.axis_index("layer"), lax.axis_index("row"), lax.axis_index("col")
    z, core = row // 2, lax.rem(row, 2)
    half = chips // 2
    owner_core = z // half
    is_owner = core == owner_core
    blocks, _, _ = out.shape
    shard = impedance.shape[1]
    sub = shard // GROUPS
    chunks = blocks * GROUPS
    rows = m_own.shape[0]
    depth = m_own.shape[1]
    sibling = (layer, z * 2 + 1 - core, col)

    def owner_of(x):
        return (layer, z * 2 + owner_core, x)

    barrier = pltpu.get_barrier_semaphore()

    def greet(device):
        pl.semaphore_signal(barrier, inc=1, device_id=device, device_id_type=MESH)

    greet(sibling)

    @pl.when(is_owner)
    def _():
        for d in range(1, cols):
            x = lax.rem(col + d, cols)
            greet((layer, z * 2, x))
            greet((layer, z * 2 + 1, x))

    @pl.when(layer > 0)
    def _():
        for k in range(half):
            greet((layer - 1, (core * half + k) * 2 + core, col))

    mine = pl.multiple_of(core * depth, LANES)
    others = pl.multiple_of((1 - core) * depth, LANES)
    load_src = pltpu.make_async_copy(sources.at[:, pl.ds(mine, depth)], src, load_sem.at[0])
    load_m = pltpu.make_async_copy(front.at[:, pl.ds(mine, depth)], m_own, load_sem.at[1])
    load_m.start()
    load_src.start()

    eye = lax.broadcasted_iota(jnp.int32, (shard, shard), 0) == lax.broadcasted_iota(jnp.int32, (shard, shard), 1)
    column = jnp.sum(jnp.where(eye, jnp.broadcast_to(impedance[...], (shard, shard)), 0.0), axis=1, keepdims=True)
    column = jnp.broadcast_to(column, (shard, LANES))
    scale[core] = pick([column[g * sub : (g + 1) * sub] for g in range(GROUPS)])

    sends_on = jnp.logical_and(is_owner, layer < layers - 1)

    @pl.when(sends_on)
    def _():
        pl.semaphore_wait(barrier, cols + chips)

    @pl.when(jnp.logical_not(sends_on))
    def _():
        pl.semaphore_wait(barrier, cols)

    swap_m = pltpu.make_async_remote_copy(
        src_ref=front.at[:, pl.ds(others, depth)], dst_ref=m_other, send_sem=swap_send.at[0], recv_sem=swap_recv.at[0],
        device_id=sibling, device_id_type=MESH)
    swap_m.start()
    swap_s = pltpu.make_async_remote_copy(
        src_ref=scale.at[core], dst_ref=scale.at[core], send_sem=swap_send.at[1], recv_sem=swap_recv.at[1],
        device_id=sibling, device_id_type=MESH)
    swap_s.start()

    load_src.wait()

    def pack_own(i, _):
        b, p = i // (2 * half), lax.rem(i, 2 * half)
        parts = [src[b, pl.ds(pl.multiple_of(p * shard + g * sub, 8), sub)] for g in range(GROUPS)]
        for q, packed in enumerate(swapped(parts)):
            own[b * GROUPS + q, pl.ds(pl.multiple_of(p * sub, 8), sub)] = packed
        return 0

    lax.fori_loop(0, blocks * 2 * half, pack_own, 0)

    @pl.when(layer == 0)
    def _():
        ag_in[...] = jnp.zeros_like(ag_in)

    def split(source, at):
        whole = source[...]
        high = whole.astype(BF16)
        m_parts[pl.ds(pl.multiple_of(at * rows, 16), rows)] = high
        m_parts[pl.ds(pl.multiple_of((2 + at) * rows, 16), rows)] = (whole - high.astype(F32)).astype(BF16)

    load_m.wait()
    split(m_own, core)
    swap_m.wait_recv()
    split(m_other, 1 - core)
    swap_s.wait_recv()

    def product(j):
        @pl.when(layer > 0)
        def _():
            pltpu.make_async_copy(ag_in.at[j], ag_in.at[j], ag_recv.at[j]).wait()

        total = own[j] + ag_in[j]
        high = total.astype(BF16).astype(F32)
        low = total - high
        highs = [turned(high, d) for d in range(GROUPS)]
        lows = [turned(low, d) for d in range(GROUPS)]
        for g in range(GROUPS):
            spread = pick([(lows if q % 2 else highs)[(q - g) % GROUPS] for q in range(GROUPS)])
            for p in range(2 * half):
                vec[pl.ds(p * shard + g * sub, sub)] = spread[p * sub : (p + 1) * sub]
        result = jnp.dot(m_parts[...], vec[...].astype(BF16), preferred_element_type=F32)
        summed = result[: 2 * rows] + result[2 * rows :]
        summed = summed + pltpu.roll(summed, WIDE, 1)
        for q in range(cols):
            for t in range(2):
                at = t * rows + q * shard
                rs_out[j, q, pl.ds(t * sub, sub)] = pick([summed[at + g * sub : at + (g + 1) * sub] for g in range(GROUPS)])
        for d in (2, 1, 3):
            x = lax.rem(col + d, cols)
            pltpu.make_async_remote_copy(
                src_ref=rs_out.at[j, x], dst_ref=rs_in.at[j, col * 2 + core], send_sem=rs_send, recv_sem=rs_recv.at[j],
                device_id=owner_of(x), device_id_type=MESH).start()

        @pl.when(jnp.logical_not(is_owner))
        def _():
            pltpu.make_async_remote_copy(
                src_ref=rs_out.at[j, col], dst_ref=rs_in.at[j, col * 2 + core], send_sem=rs_send, recv_sem=rs_recv.at[j],
                device_id=sibling, device_id_type=MESH).start()

        @pl.when(is_owner)
        def _():
            rs_in[j, col * 2 + core] = rs_out[j, col]

    def hand_on(j):
        arrived = rs_in.at[j, pl.ds(0, 2 * cols - 1)]
        pltpu.make_async_copy(arrived, arrived, rs_recv.at[j]).wait()
        total = rs_in[j, 0]
        for s in range(1, 2 * cols):
            total = total + rs_in[j, s]
        for t in range(2):
            ag_out[j, pl.ds(t * sub, sub)] = total[t * sub : (t + 1) * sub] * scale[t]

        @pl.when(layer < layers - 1)
        def _():
            for dz in (4, 3, 5, 2, 6, 1, 7, 0):
                pltpu.make_async_remote_copy(
                    src_ref=ag_out.at[j],
                    dst_ref=ag_in.at[j, pl.ds(pl.multiple_of((z - owner_core * half) * 2 * sub, 8), 2 * sub)],
                    send_sem=ag_send, recv_sem=ag_recv.at[j],
                    device_id=(layer + 1, lax.rem(z + dz, chips) * 2 + core, col), device_id_type=MESH).start()

    def tick(j, _):
        @pl.when(j < chunks)
        def _():
            product(j)

        @pl.when(jnp.logical_and(j >= LAG, is_owner))
        def _():
            hand_on(j - LAG)

        return 0

    lax.fori_loop(0, chunks + LAG, tick, 0)

    def finish(results):
        for b in range(blocks):
            for g, part in enumerate(swapped([results[b * GROUPS + q] for q in range(GROUPS)])):
                out[b, pl.ds(g * sub, sub)] = part

    @pl.when(is_owner)
    def _():
        give = pltpu.make_async_remote_copy(
            src_ref=ag_out.at[:, pl.ds(pl.multiple_of((1 - core) * sub, 8), sub)], dst_ref=from_other,
            send_sem=out_send, recv_sem=out_recv, device_id=sibling, device_id_type=MESH)
        give.start()
        kept = pl.ds(pl.multiple_of(core * sub, 8), sub)
        finish([ag_out[j, kept] for j in range(chunks)])
        give.wait_send()
        sent = rs_out.at[:, pl.ds(0, cols - 1)]
        pltpu.make_async_copy(sent, sent, rs_send).wait()

        @pl.when(layer < layers - 1)
        def _():
            pltpu.make_async_copy(rs_in, rs_in, ag_send).wait()

    @pl.when(jnp.logical_not(is_owner))
    def _():
        pltpu.make_async_copy(from_other, from_other, out_recv).wait()
        finish([from_other[j] for j in range(chunks)])
        pltpu.make_async_copy(rs_out, rs_out, rs_send).wait()

    swap_m.wait_send()
    swap_s.wait_send()


def solution(mesh):
    layers, chips, cols = mesh.shape["layer"], mesh.shape["row"] // 2, mesh.shape["col"]

    def body(front_inv, impedance, sources):
        rows, depth = front_inv.shape[1], front_inv.shape[3] // 2
        blocks, shard = sources.shape[1], impedance.shape[1]
        chunks, sub = blocks * GROUPS, shard // GROUPS
        sems = pltpu.SemaphoreType.DMA
        result = pl.pallas_call(
            functools.partial(sweep, (layers, chips, cols)),
            out_shape=jax.ShapeDtypeStruct((blocks, shard, LANES), F32),
            in_specs=[
                pl.BlockSpec(memory_space=pl.ANY),
                pl.BlockSpec(memory_space=pltpu.VMEM),
                pl.BlockSpec(memory_space=pl.ANY),
            ],
            out_specs=pl.BlockSpec(memory_space=pltpu.VMEM),
            scratch_shapes=[
                pltpu.VMEM((rows, depth), F32),
                pltpu.VMEM((rows, depth), F32),
                pltpu.VMEM((4 * rows, depth), BF16),
                pltpu.VMEM((blocks, depth, LANES), F32),
                pltpu.VMEM((chunks, chips * sub, LANES), F32),
                pltpu.VMEM((chunks, chips * sub, LANES), F32),
                pltpu.VMEM((depth, LANES), F32),
                pltpu.VMEM((chunks, cols, 2 * sub, LANES), F32),
                pltpu.VMEM((chunks, 2 * cols, 2 * sub, LANES), F32),
                pltpu.VMEM((chunks, 2 * sub, LANES), F32),
                pltpu.VMEM((chunks, sub, LANES), F32),
                pltpu.VMEM((2, sub, LANES), F32),
                sems((2,)),
                sems((2,)),
                sems((2,)),
                sems,
                sems((chunks,)),
                sems,
                sems((chunks,)),
                sems,
                sems,
            ],
            compiler_params=pltpu.CompilerParams(
                collective_id=0, has_side_effects=True, vmem_limit_bytes=40 * 2**20
            ),
            name="front_sweep",
        )(front_inv.reshape(rows, 2 * depth), impedance, sources.reshape(blocks, 2 * depth, LANES))
        return result[None]

    in_specs = (
        P("layer", "row", "col", None),
        P("layer", ("row", "col")),
        P("layer", None, "col", None, None),
    )
    out_specs = P("layer", None, ("row", "col"), None)
    return jax.shard_map(body, mesh=mesh, in_specs=in_specs, out_specs=out_specs, check_vma=False)
```

```python
import functools

import jax
import jax.numpy as jnp
from jax import lax
from jax.experimental import pallas as pl
from jax.experimental.pallas import tpu as pltpu
from jax.sharding import PartitionSpec as P

MESH = pl.DeviceIdType.MESH
F32, BF16 = jnp.float32, jnp.bfloat16
LANES = 128
HALF = LANES // 2
WIDE = 16
LAG = 3
ORDER = (2, 1, 3, 0)


def left(x, y):
    return jnp.where(lax.broadcasted_iota(jnp.int32, x.shape, 1) < HALF, x, y)


def turned(x, by):
    return pltpu.roll(x, by, 1)


def sweep(sizes, front, impedance, sources, out, tile, m_send, full, m_parts, src, own, ag_in, rs_out, rs_in, ag_out,
          from_other, raw, scale, load_sem, swap_send, swap_recv, rs_send, rs_recv, ag_send, ag_recv, out_send, out_recv):
    layers, chips, cols = sizes
    layer, row, col = lax.axis_index("layer"), lax.axis_index("row"), lax.axis_index("col")
    z, core = row // 2, lax.rem(row, 2)
    half = chips // 2
    owner_core = z // half
    is_owner = core == owner_core
    blocks, shard, _ = out.shape
    parts_of = LANES // WIDE
    chunks = blocks * parts_of
    piece = rs_in.shape[2]
    _, rows, depth = full.shape
    lane_blocks = depth // LANES
    sibling = (layer, z * 2 + 1 - core, col)

    def owner_of(x):
        return (layer, z * 2 + owner_core, x)

    barrier = pltpu.get_barrier_semaphore()

    def greet(device):
        pl.semaphore_signal(barrier, inc=1, device_id=device, device_id_type=MESH)

    @pl.when(layer > 0)
    def _():
        for k in range(half):
            greet((layer - 1, (core * half + k) * 2 + core, col))

    @pl.when(is_owner)
    def _():
        for d in range(1, cols):
            x = lax.rem(col + d, cols)
            greet((layer, z * 2, x))
            greet((layer, z * 2 + 1, x))

    greet(sibling)

    mine = pl.multiple_of(core * depth, LANES)
    load_src = pltpu.make_async_copy(sources.at[:, pl.ds(mine, depth)], src, load_sem.at[0])
    load_m = pltpu.make_async_copy(front, tile, load_sem.at[1])
    load_m.start()
    load_src.start()

    raw[core] = jnp.zeros(raw.shape[1:], F32)
    raw[core, :, :shard] = jnp.broadcast_to(impedance[...], (raw.shape[1], shard))

    def lane_block(at_core, k):
        return tile[pl.ds(at_core * lane_blocks + k, rows, stride=2 * lane_blocks)]

    load_m.wait()
    for k in range(lane_blocks):
        m_send[:, k * LANES : (k + 1) * LANES] = lane_block(1 - core, k)
    for k in range(lane_blocks):
        full[core, :, k * LANES : (k + 1) * LANES] = lane_block(core, k)

    load_src.wait()
    for b in range(blocks):
        for k in range(lane_blocks):
            if k < half:
                picked = src[b, pl.ds(2 * shard * k, LANES)]
            else:
                first = 2 * (k - half)
                picked = jnp.concatenate([src[b, pl.ds(2 * shard * i + LANES, HALF)] for i in (first, first + 1)])
            flipped = picked.T
            for c in range(parts_of):
                own[b * parts_of + c, :, k * LANES : (k + 1) * LANES] = flipped[c * WIDE : (c + 1) * WIDE]

    @pl.when(layer == 0)
    def _():
        ag_in[...] = jnp.zeros_like(ag_in)

    sends_on = jnp.logical_and(is_owner, layer < layers - 1)

    @pl.when(sends_on)
    def _():
        pl.semaphore_wait(barrier, cols + chips)

    @pl.when(jnp.logical_not(sends_on))
    def _():
        pl.semaphore_wait(barrier, cols)

    swaps = []
    for k in range(lane_blocks):
        lanes = slice(k * LANES, (k + 1) * LANES)
        swaps.append(pltpu.make_async_remote_copy(
            src_ref=m_send.at[:, lanes], dst_ref=full.at[core, :, lanes], send_sem=swap_send.at[k],
            recv_sem=swap_recv.at[k], device_id=sibling, device_id_type=MESH))
    swaps.append(pltpu.make_async_remote_copy(
        src_ref=raw.at[core], dst_ref=raw.at[core], send_sem=swap_send.at[lane_blocks],
        recv_sem=swap_recv.at[lane_blocks], device_id=sibling, device_id_type=MESH))
    for swap in swaps:
        swap.start()

    for k in range(lane_blocks):
        swaps[k].wait_recv()
        lanes = slice(k * LANES, (k + 1) * LANES)
        for pair in range(cols // 2):
            first, second = (
                pl.multiple_of(lax.rem(col + d, cols) * shard, 8) for d in ORDER[2 * pair : 2 * pair + 2])
            over = LANES - shard
            picked = [
                jnp.concatenate([full[0, pl.ds(at, shard), lanes], full[1, pl.ds(at, over), lanes]])
                for at in (first, second)
            ]
            picked.append(jnp.concatenate([full[1, pl.ds(at + over, HALF), lanes] for at in (first, second)]))
            for n, values in enumerate(picked):
                flipped = values.T
                high = flipped.astype(BF16)
                low = (flipped - high.astype(F32)).astype(BF16)
                for g in (0, 1):
                    chip, part = divmod(2 * k + g, 3)
                    to = LANES * chip + HALF * part if part < 2 else LANES * half + HALF * chip
                    for i, kept in enumerate((high, low)):
                        at = (3 * i + n) * LANES
                        m_parts[pair, to : to + HALF, at : at + LANES] = kept[g * HALF : (g + 1) * HALF]

    swaps[lane_blocks].wait_recv()
    lane = lax.broadcasted_iota(jnp.int32, raw.shape[1:], 1)
    shifted = turned(raw[1], shard)
    for at in range(0, WIDE, raw.shape[1]):
        scale[at : at + raw.shape[1]] = jnp.where(lane < shard, raw[0], shifted)
    for at in range(WIDE, piece, raw.shape[1]):
        scale[at : at + raw.shape[1]] = left(shifted, turned(shifted, HALF))

    def product(j):
        @pl.when(layer > 0)
        def _():
            pltpu.make_async_copy(ag_in.at[j], ag_in.at[j], ag_recv.at[j]).wait()

        came = [ag_in[j, k, :WIDE] for k in range(half)]
        for k in range(0, half, 2):
            a, b = ag_in[j, k, WIDE:], ag_in[j, k + 1, WIDE:]
            came.append(jnp.concatenate([left(a, turned(b, HALF)), left(turned(a, HALF), b)]))
        total = own[j] + jnp.concatenate(came, axis=1)
        high = total.astype(BF16)
        vec = jnp.concatenate([high, (total - high.astype(F32)).astype(BF16)])
        for pair in range(cols // 2):
            result = jnp.dot(vec, m_parts[pair], preferred_element_type=F32)
            result = result[:WIDE] + result[WIDE:]
            result = result[:, : 3 * LANES] + result[:, 3 * LANES :]
            top, bottom = result[: WIDE // 2, 2 * LANES :], result[WIDE // 2 :, 2 * LANES :]
            rs_out[j, 2 * pair, :WIDE] = result[:, :LANES]
            rs_out[j, 2 * pair, WIDE:] = left(top, turned(bottom, HALF))
            rs_out[j, 2 * pair + 1, :WIDE] = result[:, LANES : 2 * LANES]
            rs_out[j, 2 * pair + 1, WIDE:] = left(turned(top, HALF), bottom)
            for n in (2 * pair, 2 * pair + 1):
                if ORDER[n]:
                    pltpu.make_async_remote_copy(
                        src_ref=rs_out.at[j, n], dst_ref=rs_in.at[j, col * 2 + core], send_sem=rs_send,
                        recv_sem=rs_recv.at[j], device_id=owner_of(lax.rem(col + ORDER[n], cols)),
                        device_id_type=MESH).start()

        @pl.when(jnp.logical_not(is_owner))
        def _():
            pltpu.make_async_remote_copy(
                src_ref=rs_out.at[j, cols - 1], dst_ref=rs_in.at[j, col * 2 + core], send_sem=rs_send,
                recv_sem=rs_recv.at[j], device_id=sibling, device_id_type=MESH).start()

        @pl.when(is_owner)
        def _():
            rs_in[j, col * 2 + core] = rs_out[j, cols - 1]

    def hand_on(j):
        arrived = rs_in.at[j, pl.ds(0, 2 * cols - 1)]
        pltpu.make_async_copy(arrived, arrived, rs_recv.at[j]).wait()
        total = rs_in[j, 0]
        for s in range(1, 2 * cols):
            total = total + rs_in[j, s]
        ag_out[j] = total * scale[...]

        @pl.when(layer < layers - 1)
        def _():
            for dz in (4, 3, 5, 2, 6, 1, 7, 0):
                pltpu.make_async_remote_copy(
                    src_ref=ag_out.at[j], dst_ref=ag_in.at[j, z - owner_core * half],
                    send_sem=ag_send, recv_sem=ag_recv.at[j],
                    device_id=(layer + 1, lax.rem(z + dz, chips) * 2 + core, col), device_id_type=MESH).start()

    def tick(j, _):
        @pl.when(j < chunks)
        def _():
            product(j)

        @pl.when(jnp.logical_and(j >= LAG, is_owner))
        def _():
            hand_on(j - LAG)

        return 0

    lax.fori_loop(0, chunks + LAG, tick, 0)

    def finish(results):
        for b in range(blocks):
            some = [results[b * parts_of + c] for c in range(parts_of)]
            first = jnp.concatenate([r[:WIDE] for r in some])
            rest = jnp.concatenate([v for r in some for v in (r[WIDE:], turned(r[WIDE:], HALF))])
            lane = lax.broadcasted_iota(jnp.int32, first.shape, 1)
            over = LANES - shard
            second = jnp.where(lane < over, turned(first, over), turned(rest, over))
            out[b] = jnp.where(core == 0, first, second).T[:shard]

    @pl.when(is_owner)
    def _():
        give = pltpu.make_async_remote_copy(
            src_ref=ag_out, dst_ref=from_other, send_sem=out_send, recv_sem=out_recv, device_id=sibling,
            device_id_type=MESH)
        give.start()
        finish([ag_out[j] for j in range(chunks)])
        give.wait_send()
        sent = rs_out.at[:, pl.ds(0, cols - 1)]
        pltpu.make_async_copy(sent, sent, rs_send).wait()

        @pl.when(layer < layers - 1)
        def _():
            pltpu.make_async_copy(rs_in, rs_in, ag_send).wait()

    @pl.when(jnp.logical_not(is_owner))
    def _():
        pltpu.make_async_copy(from_other, from_other, out_recv).wait()
        finish([from_other[j] for j in range(chunks)])
        pltpu.make_async_copy(rs_out, rs_out, rs_send).wait()

    for swap in swaps:
        swap.wait_send()


def solution(mesh):
    layers, chips, cols = mesh.shape["layer"], mesh.shape["row"] // 2, mesh.shape["col"]

    def body(front_inv, impedance, sources):
        rows, depth = front_inv.shape[1], front_inv.shape[3] // 2
        blocks, shard = sources.shape[1], impedance.shape[1]
        chunks, piece = blocks * LANES // WIDE, 2 * shard * WIDE // LANES
        sems = pltpu.SemaphoreType.DMA
        result = pl.pallas_call(
            functools.partial(sweep, (layers, chips, cols)),
            out_shape=jax.ShapeDtypeStruct((blocks, shard, LANES), F32),
            in_specs=[
                pl.BlockSpec(memory_space=pl.ANY),
                pl.BlockSpec(memory_space=pltpu.VMEM),
                pl.BlockSpec(memory_space=pl.ANY),
            ],
            out_specs=pl.BlockSpec(memory_space=pltpu.VMEM),
            scratch_shapes=[
                pltpu.VMEM((rows * 2 * depth // LANES, LANES), F32),
                pltpu.VMEM((rows, depth), F32),
                pltpu.VMEM((2, rows, depth), F32),
                pltpu.VMEM((cols // 2, depth, 2 * rows), BF16),
                pltpu.VMEM((blocks, depth, LANES), F32),
                pltpu.VMEM((chunks, WIDE, depth), F32),
                pltpu.VMEM((chunks, chips // 2, piece, LANES), F32),
                pltpu.VMEM((chunks, cols, piece, LANES), F32),
                pltpu.VMEM((chunks, 2 * cols, piece, LANES), F32),
                pltpu.VMEM((chunks, piece, LANES), F32),
                pltpu.VMEM((chunks, piece, LANES), F32),
                pltpu.VMEM((2, 8, LANES), F32),
                pltpu.VMEM((piece, LANES), F32),
                sems((2,)),
                sems((depth // LANES + 1,)),
                sems((depth // LANES + 1,)),
                sems,
                sems((chunks,)),
                sems,
                sems((chunks,)),
                sems,
                sems,
            ],
            compiler_params=pltpu.CompilerParams(
                collective_id=0, has_side_effects=True, vmem_limit_bytes=56 * 2**20
            ),
            name="front_sweep",
        )(
            front_inv.reshape(rows * 2 * depth // LANES, LANES),
            impedance,
            sources.reshape(blocks, 2 * depth, LANES),
        )
        return result[None]

    in_specs = (
        P("layer", "row", "col", None),
        P("layer", ("row", "col")),
        P("layer", None, "col", None, None),
    )
    out_specs = P("layer", None, ("row", "col"), None)
    return jax.shard_map(body, mesh=mesh, in_specs=in_specs, out_specs=out_specs, check_vma=False)
```

```python
import functools

import jax
import jax.numpy as jnp
from jax import lax
from jax.experimental import pallas as pl
from jax.experimental.pallas import tpu as pltpu
from jax.sharding import PartitionSpec as P

MESH = pl.DeviceIdType.MESH
F32, BF16 = jnp.float32, jnp.bfloat16
LANES = 128
HALF = LANES // 2
WIDE = 16
LAG = 3
ORDER = (2, 1, 3, 0)
SPREAD = (4, 3, 5, 2, 6, 1, 7, 0)


def left(x, y):
    return jnp.where(lax.broadcasted_iota(jnp.int32, x.shape, 1) < HALF, x, y)


def turned(x, by):
    return pltpu.roll(x, by, 1)


def sweep(sizes, front, impedance, sources, out, tile, m_send, full, m_parts, src, own, ag_in, rs_out, rs_in, ag_out,
          raw, scale, ready, load_sem, swap_send, swap_recv, rs_send, rs_recv, ag_send, ag_recv, out_send, out_recv):
    layers, chips, cols = sizes
    layer, row, col = lax.axis_index("layer"), lax.axis_index("row"), lax.axis_index("col")
    z, core = row // 2, lax.rem(row, 2)
    half = chips // 2
    half_of = z // half
    blocks, shard, _ = out.shape
    parts_of = LANES // WIDE
    chunks = blocks * parts_of
    piece = rs_in.shape[2]
    _, rows, depth = full.shape
    lane_blocks = depth // LANES
    sibling = (layer, z * 2 + 1 - core, col)

    is_owner = core == half_of

    barrier = pltpu.get_barrier_semaphore()

    def greet(device):
        pl.semaphore_signal(barrier, inc=1, device_id=device, device_id_type=MESH)

    hands_on = jnp.logical_and(is_owner, layer < layers - 1)

    @pl.when(hands_on)
    def _():
        for dz in SPREAD:
            greet((layer + 1, lax.rem(z + dz, chips) * 2 + core, col))

    @pl.when(is_owner)
    def _():
        for d in ORDER[:-1]:
            x = lax.rem(col + d, cols)
            greet((layer, z * 2, x))
            greet((layer, z * 2 + 1, x))

    greet(sibling)

    mine = pl.multiple_of(core * depth, LANES)
    load_src = pltpu.make_async_copy(sources.at[:, pl.ds(mine, depth)], src, load_sem.at[0])
    load_m = pltpu.make_async_copy(front, tile, load_sem.at[1])
    load_m.start()
    load_src.start()

    raw[core] = jnp.zeros(raw.shape[1:], F32)
    raw[core, :, :shard] = jnp.broadcast_to(impedance[...], (raw.shape[1], shard))

    def lane_block(at_core, k):
        return tile[pl.ds(at_core * lane_blocks + k, rows, stride=2 * lane_blocks)]

    load_m.wait()
    for k in range(lane_blocks):
        m_send[:, k * LANES : (k + 1) * LANES] = lane_block(1 - core, k)
    for k in range(lane_blocks):
        full[core, :, k * LANES : (k + 1) * LANES] = lane_block(core, k)

    @pl.when(layer == 0)
    def _():
        ag_in[...] = jnp.zeros_like(ag_in)

    @pl.when(layer == 0)
    def _():
        pl.semaphore_wait(barrier, cols)

    @pl.when(layer > 0)
    def _():
        pl.semaphore_wait(barrier, cols + half)
        for k in range(half):
            pl.semaphore_signal(
                ready, inc=1, device_id=(layer - 1, (core * half + k) * 2 + core, col), device_id_type=MESH)

    swaps = []
    for k in range(lane_blocks):
        lanes = slice(k * LANES, (k + 1) * LANES)
        swaps.append(pltpu.make_async_remote_copy(
            src_ref=m_send.at[:, lanes], dst_ref=full.at[core, :, lanes], send_sem=swap_send.at[k],
            recv_sem=swap_recv.at[k], device_id=sibling, device_id_type=MESH))
    swaps.append(pltpu.make_async_remote_copy(
        src_ref=raw.at[core], dst_ref=raw.at[core], send_sem=swap_send.at[lane_blocks],
        recv_sem=swap_recv.at[lane_blocks], device_id=sibling, device_id_type=MESH))
    for swap in swaps:
        swap.start()

    load_src.wait()
    for b in range(blocks):
        for k in range(lane_blocks):
            if k < half:
                picked = src[b, pl.ds(2 * shard * k, LANES)]
            else:
                first = 2 * (k - half)
                picked = jnp.concatenate([src[b, pl.ds(2 * shard * i + LANES, HALF)] for i in (first, first + 1)])
            flipped = picked.T
            for c in range(parts_of):
                own[b * parts_of + c, :, k * LANES : (k + 1) * LANES] = flipped[c * WIDE : (c + 1) * WIDE]

    for k in range(lane_blocks):
        swaps[k].wait_recv()
        lanes = slice(k * LANES, (k + 1) * LANES)
        for pair in range(cols // 2):
            first, second = (
                pl.multiple_of(lax.rem(col + d, cols) * shard, 8) for d in ORDER[2 * pair : 2 * pair + 2])
            over = LANES - shard
            picked = [
                jnp.concatenate([full[0, pl.ds(at, shard), lanes], full[1, pl.ds(at, over), lanes]])
                for at in (first, second)
            ]
            picked.append(jnp.concatenate([full[1, pl.ds(at + over, HALF), lanes] for at in (first, second)]))
            for n, values in enumerate(picked):
                flipped = values.T
                high = flipped.astype(BF16)
                low = (flipped - high.astype(F32)).astype(BF16)
                for g in (0, 1):
                    chip, part = divmod(2 * k + g, 3)
                    to = LANES * chip + HALF * part if part < 2 else LANES * half + HALF * chip
                    for i, kept in enumerate((high, low)):
                        at = (3 * i + n) * LANES
                        m_parts[pair, to : to + HALF, at : at + LANES] = kept[g * HALF : (g + 1) * HALF]

    swaps[lane_blocks].wait_recv()
    lane = lax.broadcasted_iota(jnp.int32, raw.shape[1:], 1)
    shifted = turned(raw[1], shard)
    for at in range(0, WIDE, raw.shape[1]):
        scale[at : at + raw.shape[1]] = jnp.where(lane < shard, raw[0], shifted)
    for at in range(WIDE, piece, raw.shape[1]):
        scale[at : at + raw.shape[1]] = left(shifted, turned(shifted, HALF))

    def product(j):
        @pl.when(layer > 0)
        def _():
            pltpu.make_async_copy(ag_in.at[j], ag_in.at[j], ag_recv.at[j]).wait()

        came = [ag_in[j, k, :WIDE] for k in range(half)]
        for k in range(0, half, 2):
            a, b = ag_in[j, k, WIDE:], ag_in[j, k + 1, WIDE:]
            came.append(jnp.concatenate([left(a, turned(b, HALF)), left(turned(a, HALF), b)]))
        total = own[j] + jnp.concatenate(came, axis=1)
        high = total.astype(BF16)
        vec = jnp.concatenate([high, (total - high.astype(F32)).astype(BF16)])
        for pair in range(cols // 2):
            result = jnp.dot(vec, m_parts[pair], preferred_element_type=F32)
            result = result[:WIDE] + result[WIDE:]
            result = result[:, : 3 * LANES] + result[:, 3 * LANES :]
            top, bottom = result[: WIDE // 2, 2 * LANES :], result[WIDE // 2 :, 2 * LANES :]
            rs_out[j, 2 * pair, :WIDE] = result[:, :LANES]
            rs_out[j, 2 * pair, WIDE:] = left(top, turned(bottom, HALF))
            rs_out[j, 2 * pair + 1, :WIDE] = result[:, LANES : 2 * LANES]
            rs_out[j, 2 * pair + 1, WIDE:] = left(turned(top, HALF), bottom)
            for n in (2 * pair, 2 * pair + 1):
                if ORDER[n]:
                    pltpu.make_async_remote_copy(
                        src_ref=rs_out.at[j, n], dst_ref=rs_in.at[j, col * 2 + core], send_sem=rs_send,
                        recv_sem=rs_recv.at[j], device_id=(layer, z * 2 + half_of, lax.rem(col + ORDER[n], cols)),
                        device_id_type=MESH).start()

        @pl.when(jnp.logical_not(is_owner))
        def _():
            pltpu.make_async_remote_copy(
                src_ref=rs_out.at[j, cols - 1], dst_ref=rs_in.at[j, col * 2 + core], send_sem=rs_send,
                recv_sem=rs_recv.at[j], device_id=sibling, device_id_type=MESH).start()

        @pl.when(is_owner)
        def _():
            rs_in[j, col * 2 + core] = rs_out[j, cols - 1]

    def give(b):
        some = ag_out.at[pl.ds(b * parts_of, parts_of)]
        return pltpu.make_async_remote_copy(
            src_ref=some, dst_ref=some, send_sem=out_send.at[b], recv_sem=out_recv.at[b], device_id=sibling,
            device_id_type=MESH)

    def hand_on(j):
        arrived = rs_in.at[j, pl.ds(0, 2 * cols - 1)]
        pltpu.make_async_copy(arrived, arrived, rs_recv.at[j]).wait()
        total = rs_in[j, 0]
        for s in range(1, 2 * cols):
            total = total + rs_in[j, s]
        ag_out[j] = total * scale[...]

        @pl.when(layer < layers - 1)
        def _():
            @pl.when(j == 0)
            def _():
                pl.semaphore_wait(ready, chips)

            for dz in SPREAD:
                pltpu.make_async_remote_copy(
                    src_ref=ag_out.at[j], dst_ref=ag_in.at[j, z - half_of * half],
                    send_sem=ag_send, recv_sem=ag_recv.at[j],
                    device_id=(layer + 1, lax.rem(z + dz, chips) * 2 + half_of, col), device_id_type=MESH).start()

        @pl.when(lax.rem(j, parts_of) == parts_of - 1)
        def _():
            give(j // parts_of).start()

    def tick(j, _):
        @pl.when(j < chunks)
        def _():
            product(j)

        @pl.when(jnp.logical_and(j >= LAG, is_owner))
        def _():
            hand_on(j - LAG)

        return 0

    lax.fori_loop(0, chunks + LAG, tick, 0)

    for b in range(blocks):
        @pl.when(jnp.logical_not(is_owner))
        def _():
            give(b).wait_recv()

        some = [ag_out[j] for j in range(b * parts_of, (b + 1) * parts_of)]
        first = jnp.concatenate([r[:WIDE] for r in some])
        rest = jnp.concatenate([v for r in some for v in (r[WIDE:], turned(r[WIDE:], HALF))])
        lane = lax.broadcasted_iota(jnp.int32, first.shape, 1)
        over = LANES - shard
        second = jnp.where(lane < over, turned(first, over), turned(rest, over))
        out[b] = jnp.where(core == 0, first, second).T[:shard]

    @pl.when(jnp.logical_not(is_owner))
    def _():
        pltpu.make_async_copy(rs_out, rs_out, rs_send).wait()

    @pl.when(is_owner)
    def _():
        for b in range(blocks):
            give(b).wait_send()
        sent = rs_out.at[:, pl.ds(0, cols - 1)]
        pltpu.make_async_copy(sent, sent, rs_send).wait()

    @pl.when(hands_on)
    def _():
        pltpu.make_async_copy(rs_in, rs_in, ag_send).wait()

    for swap in swaps:
        swap.wait_send()


def solution(mesh):
    layers, chips, cols = mesh.shape["layer"], mesh.shape["row"] // 2, mesh.shape["col"]

    def body(front_inv, impedance, sources):
        rows, depth = front_inv.shape[1], front_inv.shape[3] // 2
        blocks, shard = sources.shape[1], impedance.shape[1]
        chunks, piece = blocks * LANES // WIDE, 2 * shard * WIDE // LANES
        sems = pltpu.SemaphoreType.DMA
        result = pl.pallas_call(
            functools.partial(sweep, (layers, chips, cols)),
            out_shape=jax.ShapeDtypeStruct((blocks, shard, LANES), F32),
            in_specs=[
                pl.BlockSpec(memory_space=pl.ANY),
                pl.BlockSpec(memory_space=pltpu.VMEM),
                pl.BlockSpec(memory_space=pl.ANY),
            ],
            out_specs=pl.BlockSpec(memory_space=pltpu.VMEM),
            scratch_shapes=[
                pltpu.VMEM((rows * 2 * depth // LANES, LANES), F32),
                pltpu.VMEM((rows, depth), F32),
                pltpu.VMEM((2, rows, depth), F32),
                pltpu.VMEM((cols // 2, depth, 2 * rows), BF16),
                pltpu.VMEM((blocks, depth, LANES), F32),
                pltpu.VMEM((chunks, WIDE, depth), F32),
                pltpu.VMEM((chunks, chips // 2, piece, LANES), F32),
                pltpu.VMEM((chunks, cols, piece, LANES), F32),
                pltpu.VMEM((chunks, 2 * cols, piece, LANES), F32),
                pltpu.VMEM((chunks, piece, LANES), F32),
                pltpu.VMEM((2, 8, LANES), F32),
                pltpu.VMEM((piece, LANES), F32),
                pltpu.SemaphoreType.REGULAR,
                sems((2,)),
                sems((depth // LANES + 1,)),
                sems((depth // LANES + 1,)),
                sems,
                sems((chunks,)),
                sems,
                sems((chunks,)),
                sems((blocks,)),
                sems((blocks,)),
            ],
            compiler_params=pltpu.CompilerParams(
                collective_id=0, has_side_effects=True, vmem_limit_bytes=52 * 2**20
            ),
            name="front_sweep",
        )(
            front_inv.reshape(rows * 2 * depth // LANES, LANES),
            impedance,
            sources.reshape(blocks, 2 * depth, LANES),
        )
        return result[None]

    in_specs = (
        P("layer", "row", "col", None),
        P("layer", ("row", "col")),
        P("layer", None, "col", None, None),
    )
    out_specs = P("layer", None, ("row", "col"), None)
    return jax.shard_map(body, mesh=mesh, in_specs=in_specs, out_specs=out_specs, check_vma=False)
```

```python
import functools

import jax
import jax.numpy as jnp
from jax import lax
from jax.experimental import pallas as pl
from jax.experimental.pallas import tpu as pltpu
from jax.sharding import PartitionSpec as P

MESH = pl.DeviceIdType.MESH
F32, BF16 = jnp.float32, jnp.bfloat16
LANES = 128
HALF = LANES // 2
WIDE = 16
LAG = 3
ORDER = (2, 1, 3, 0)
SPREAD = (4, 3, 5, 2, 6, 1, 7, 0)


def left(x, y):
    return jnp.where(lax.broadcasted_iota(jnp.int32, x.shape, 1) < HALF, x, y)


def turned(x, by):
    return pltpu.roll(x, by, 1)


def sweep(sizes, front, impedance, sources, out, tile, m_send, full, m_parts, src, own, ag_in, rs_out, rs_in, ag_out,
          raw, scale, ready, load_sem, swap_send, swap_recv, rs_send, rs_recv, ag_send, ag_recv, out_send, out_recv):
    layers, chips, cols = sizes
    layer, row, col = lax.axis_index("layer"), lax.axis_index("row"), lax.axis_index("col")
    z, core = row // 2, lax.rem(row, 2)
    half = chips // 2
    half_of = z // half
    blocks, shard, _ = out.shape
    parts_of = LANES // WIDE
    chunks = blocks * parts_of
    piece = rs_in.shape[2]
    _, rows, depth = full.shape
    lane_blocks = depth // LANES
    sibling = (layer, z * 2 + 1 - core, col)

    is_owner = core == half_of

    barrier = pltpu.get_barrier_semaphore()

    def greet(device):
        pl.semaphore_signal(barrier, inc=1, device_id=device, device_id_type=MESH)

    hands_on = jnp.logical_and(is_owner, layer < layers - 1)

    @pl.when(hands_on)
    def _():
        for dz in SPREAD:
            greet((layer + 1, lax.rem(z + dz, chips) * 2 + core, col))

    @pl.when(is_owner)
    def _():
        for d in ORDER[:-1]:
            x = lax.rem(col + d, cols)
            greet((layer, z * 2, x))
            greet((layer, z * 2 + 1, x))

    greet(sibling)

    mine = pl.multiple_of(core * depth, LANES)
    load_src = pltpu.make_async_copy(sources.at[:, pl.ds(mine, depth)], src, load_sem.at[0])
    load_m = pltpu.make_async_copy(front, tile.at[pl.ds(0, front.shape[0])], load_sem.at[1])
    load_m.start()
    load_src.start()

    raw[core] = jnp.zeros(raw.shape[1:], F32)
    raw[core, :, :shard] = jnp.broadcast_to(impedance[...], (raw.shape[1], shard))

    def lane_block(at_core, k):
        return tile[pl.ds(at_core * lane_blocks + k, rows, stride=2 * lane_blocks)]

    load_m.wait()
    for k in range(lane_blocks):
        m_send[:, k * LANES : (k + 1) * LANES] = lane_block(1 - core, k)
    for k in range(lane_blocks):
        full[core, :, k * LANES : (k + 1) * LANES] = lane_block(core, k)

    @pl.when(layer == 0)
    def _():
        ag_in[...] = jnp.zeros_like(ag_in)

    @pl.when(layer == 0)
    def _():
        pl.semaphore_wait(barrier, cols)

    @pl.when(layer > 0)
    def _():
        pl.semaphore_wait(barrier, cols + half)
        for k in range(half):
            pl.semaphore_signal(
                ready, inc=1, device_id=(layer - 1, (core * half + k) * 2 + core, col), device_id_type=MESH)

    swaps = []
    for k in range(lane_blocks):
        lanes = slice(k * LANES, (k + 1) * LANES)
        swaps.append(pltpu.make_async_remote_copy(
            src_ref=m_send.at[:, lanes], dst_ref=full.at[core, :, lanes], send_sem=swap_send.at[k],
            recv_sem=swap_recv.at[k], device_id=sibling, device_id_type=MESH))
    swaps.append(pltpu.make_async_remote_copy(
        src_ref=raw.at[core], dst_ref=raw.at[core], send_sem=swap_send.at[lane_blocks],
        recv_sem=swap_recv.at[lane_blocks], device_id=sibling, device_id_type=MESH))
    for swap in swaps:
        swap.start()

    load_src.wait()
    for b in range(blocks):
        for k in range(lane_blocks):
            if k < half:
                picked = src[b, pl.ds(2 * shard * k, LANES)]
            else:
                first = 2 * (k - half)
                picked = jnp.concatenate([src[b, pl.ds(2 * shard * i + LANES, HALF)] for i in (first, first + 1)])
            flipped = picked.T
            for c in range(parts_of):
                own[b * parts_of + c, :, k * LANES : (k + 1) * LANES] = flipped[c * WIDE : (c + 1) * WIDE]

    for k in range(lane_blocks):
        swaps[k].wait_recv()
        lanes = slice(k * LANES, (k + 1) * LANES)
        for pair in range(cols // 2):
            first, second = (
                pl.multiple_of(lax.rem(col + d, cols) * shard, 8) for d in ORDER[2 * pair : 2 * pair + 2])
            over = LANES - shard
            picked = [
                jnp.concatenate([full[0, pl.ds(at, shard), lanes], full[1, pl.ds(at, over), lanes]])
                for at in (first, second)
            ]
            picked.append(jnp.concatenate([full[1, pl.ds(at + over, HALF), lanes] for at in (first, second)]))
            for n, values in enumerate(picked):
                flipped = values.T
                high = flipped.astype(BF16)
                low = (flipped - high.astype(F32)).astype(BF16)
                for g in (0, 1):
                    chip, part = divmod(2 * k + g, 3)
                    to = LANES * chip + HALF * part if part < 2 else LANES * half + HALF * chip
                    for i, kept in enumerate((high, low)):
                        at = (3 * i + n) * LANES
                        m_parts[pair, to : to + HALF, at : at + LANES] = kept[g * HALF : (g + 1) * HALF]

    swaps[lane_blocks].wait_recv()
    lane = lax.broadcasted_iota(jnp.int32, raw.shape[1:], 1)
    shifted = turned(raw[1], shard)
    for at in range(0, WIDE, raw.shape[1]):
        scale[at : at + raw.shape[1]] = jnp.where(lane < shard, raw[0], shifted)
    for at in range(WIDE, piece, raw.shape[1]):
        scale[at : at + raw.shape[1]] = left(shifted, turned(shifted, HALF))

    def product(j):
        @pl.when(layer > 0)
        def _():
            pltpu.make_async_copy(ag_in.at[j], ag_in.at[j], ag_recv.at[j]).wait()

        came = [ag_in[j, k, :WIDE] for k in range(half)]
        for k in range(0, half, 2):
            a, b = ag_in[j, k, WIDE:], ag_in[j, k + 1, WIDE:]
            came.append(jnp.concatenate([left(a, turned(b, HALF)), left(turned(a, HALF), b)]))
        total = own[j] + jnp.concatenate(came, axis=1)
        high = total.astype(BF16)
        vec = jnp.concatenate([high, (total - high.astype(F32)).astype(BF16)])
        for pair in range(cols // 2):
            result = jnp.dot(vec, m_parts[pair], preferred_element_type=F32)
            result = result[:WIDE] + result[WIDE:]
            result = result[:, : 3 * LANES] + result[:, 3 * LANES :]
            top, bottom = result[: WIDE // 2, 2 * LANES :], result[WIDE // 2 :, 2 * LANES :]
            rs_out[j, 2 * pair, :WIDE] = result[:, :LANES]
            rs_out[j, 2 * pair, WIDE:] = left(top, turned(bottom, HALF))
            rs_out[j, 2 * pair + 1, :WIDE] = result[:, LANES : 2 * LANES]
            rs_out[j, 2 * pair + 1, WIDE:] = left(turned(top, HALF), bottom)
            for n in (2 * pair, 2 * pair + 1):
                if ORDER[n]:
                    pltpu.make_async_remote_copy(
                        src_ref=rs_out.at[j, n], dst_ref=rs_in.at[j, col * 2 + core], send_sem=rs_send,
                        recv_sem=rs_recv.at[j], device_id=(layer, z * 2 + half_of, lax.rem(col + ORDER[n], cols)),
                        device_id_type=MESH).start()

        @pl.when(jnp.logical_not(is_owner))
        def _():
            pltpu.make_async_remote_copy(
                src_ref=rs_out.at[j, cols - 1], dst_ref=rs_in.at[j, col * 2 + core], send_sem=rs_send,
                recv_sem=rs_recv.at[j], device_id=sibling, device_id_type=MESH).start()

        @pl.when(is_owner)
        def _():
            rs_in[j, col * 2 + core] = rs_out[j, cols - 1]

    def give(b):
        some = ag_out.at[pl.ds(b * parts_of, parts_of)]
        return pltpu.make_async_remote_copy(
            src_ref=some, dst_ref=some, send_sem=out_send.at[b], recv_sem=out_recv.at[b], device_id=sibling,
            device_id_type=MESH)

    def hand_on(j):
        arrived = rs_in.at[j, pl.ds(0, 2 * cols - 1)]
        pltpu.make_async_copy(arrived, arrived, rs_recv.at[j]).wait()
        total = rs_in[j, 0]
        for s in range(1, 2 * cols):
            total = total + rs_in[j, s]
        ag_out[j] = total * scale[...]

        @pl.when(layer < layers - 1)
        def _():
            @pl.when(j == 0)
            def _():
                pl.semaphore_wait(ready, chips)

            for dz in SPREAD:
                pltpu.make_async_remote_copy(
                    src_ref=ag_out.at[j], dst_ref=ag_in.at[j, z - half_of * half],
                    send_sem=ag_send, recv_sem=ag_recv.at[j],
                    device_id=(layer + 1, lax.rem(z + dz, chips) * 2 + half_of, col), device_id_type=MESH).start()

        @pl.when(lax.rem(j, parts_of) == parts_of - 1)
        def _():
            give(j // parts_of).start()

    def tick(j, _):
        @pl.when(j < chunks)
        def _():
            product(j)

        @pl.when(jnp.logical_and(j >= LAG, is_owner))
        def _():
            hand_on(j - LAG)

        return 0

    lax.fori_loop(0, chunks + LAG, tick, 0)

    for b in range(blocks):
        @pl.when(jnp.logical_not(is_owner))
        def _():
            give(b).wait_recv()

        some = [ag_out[j] for j in range(b * parts_of, (b + 1) * parts_of)]
        first = jnp.concatenate([r[:WIDE] for r in some])
        rest = jnp.concatenate([v for r in some for v in (r[WIDE:], turned(r[WIDE:], HALF))])
        lane = lax.broadcasted_iota(jnp.int32, first.shape, 1)
        over = LANES - shard
        second = jnp.where(lane < over, turned(first, over), turned(rest, over))
        out[b] = jnp.where(core == 0, first, second).T[:shard]

    @pl.when(jnp.logical_not(is_owner))
    def _():
        pltpu.make_async_copy(rs_out, rs_out, rs_send).wait()

    @pl.when(is_owner)
    def _():
        for b in range(blocks):
            give(b).wait_send()
        sent = rs_out.at[:, pl.ds(0, cols - 1)]
        pltpu.make_async_copy(sent, sent, rs_send).wait()

    @pl.when(hands_on)
    def _():
        pltpu.make_async_copy(rs_in, rs_in, ag_send).wait()

    for swap in swaps:
        swap.wait_send()


def solution(mesh):
    layers, chips, cols = mesh.shape["layer"], mesh.shape["row"] // 2, mesh.shape["col"]

    def body(front_inv, impedance, sources):
        rows, depth = front_inv.shape[1], front_inv.shape[3] // 2
        blocks, shard = sources.shape[1], impedance.shape[1]
        chunks, piece = blocks * LANES // WIDE, 2 * shard * WIDE // LANES
        sems = pltpu.SemaphoreType.DMA
        result = pl.pallas_call(
            functools.partial(sweep, (layers, chips, cols)),
            out_shape=jax.ShapeDtypeStruct((blocks, shard, LANES), F32),
            in_specs=[
                pl.BlockSpec(memory_space=pl.ANY),
                pl.BlockSpec(memory_space=pltpu.VMEM),
                pl.BlockSpec(memory_space=pl.ANY),
            ],
            out_specs=pl.BlockSpec(memory_space=pltpu.VMEM),
            scratch_shapes=[
                pltpu.VMEM((rows * 2 * depth // LANES + 16, LANES), F32),
                pltpu.VMEM((rows, depth), F32),
                pltpu.VMEM((2, rows, depth), F32),
                pltpu.VMEM((cols // 2, depth, 2 * rows), BF16),
                pltpu.VMEM((blocks, depth, LANES), F32),
                pltpu.VMEM((chunks, WIDE, depth), F32),
                pltpu.VMEM((chunks, chips // 2, piece, LANES), F32),
                pltpu.VMEM((chunks, cols, piece, LANES), F32),
                pltpu.VMEM((chunks, 2 * cols, piece, LANES), F32),
                pltpu.VMEM((chunks, piece, LANES), F32),
                pltpu.VMEM((2, 8, LANES), F32),
                pltpu.VMEM((piece, LANES), F32),
                pltpu.SemaphoreType.REGULAR,
                sems((2,)),
                sems((depth // LANES + 1,)),
                sems((depth // LANES + 1,)),
                sems,
                sems((chunks,)),
                sems,
                sems((chunks,)),
                sems((blocks,)),
                sems((blocks,)),
            ],
            compiler_params=pltpu.CompilerParams(
                collective_id=0, has_side_effects=True, vmem_limit_bytes=52 * 2**20
            ),
            name="front_sweep",
        )(
            front_inv.reshape(rows * 2 * depth // LANES, LANES),
            impedance,
            sources.reshape(blocks, 2 * depth, LANES),
        )
        return result[None]

    in_specs = (
        P("layer", "row", "col", None),
        P("layer", ("row", "col")),
        P("layer", None, "col", None, None),
    )
    out_specs = P("layer", None, ("row", "col"), None)
    return jax.shard_map(body, mesh=mesh, in_specs=in_specs, out_specs=out_specs, check_vma=False)
```

```python
import functools

import jax
import jax.numpy as jnp
from jax import lax
from jax.experimental import pallas as pl
from jax.experimental.pallas import tpu as pltpu
from jax.sharding import PartitionSpec as P

MESH = pl.DeviceIdType.MESH
F32, BF16 = jnp.float32, jnp.bfloat16
LANES = 128
HALF = LANES // 2
WIDE = 16
LAG = 3
ORDER = (2, 1, 3, 0)
SPREAD = (4, 3, 5, 2, 6, 1, 7, 0)


def left(x, y):
    return jnp.where(lax.broadcasted_iota(jnp.int32, x.shape, 1) < HALF, x, y)


def turned(x, by):
    return pltpu.roll(x, by, 1)


def sweep(sizes, front, impedance, sources, out, tile, m_send, full, m_parts, src, own, ag_in, rs_out, rs_in, ag_out,
          raw, scale, ready, load_sem, swap_send, swap_recv, rs_send, rs_recv, ag_send, ag_recv, out_send, out_recv):
    layers, chips, cols = sizes
    layer, row, col = lax.axis_index("layer"), lax.axis_index("row"), lax.axis_index("col")
    z, core = row // 2, lax.rem(row, 2)
    half = chips // 2
    half_of = z // half
    blocks, shard, _ = out.shape
    parts_of = LANES // WIDE
    chunks = blocks * parts_of
    piece = rs_in.shape[2]
    _, rows, depth = full.shape
    lane_blocks = depth // LANES
    sibling = (layer, z * 2 + 1 - core, col)

    is_owner = core == half_of

    barrier = pltpu.get_barrier_semaphore()

    def greet(device):
        pl.semaphore_signal(barrier, inc=1, device_id=device, device_id_type=MESH)

    hands_on = jnp.logical_and(is_owner, layer < layers - 1)

    @pl.when(hands_on)
    def _():
        for dz in SPREAD:
            greet((layer + 1, lax.rem(z + dz, chips) * 2 + core, col))

    @pl.when(is_owner)
    def _():
        for d in ORDER[:-1]:
            x = lax.rem(col + d, cols)
            greet((layer, z * 2, x))
            greet((layer, z * 2 + 1, x))

    greet(sibling)

    mine = pl.multiple_of(core * depth, LANES)
    load_src = pltpu.make_async_copy(sources.at[:, pl.ds(mine, depth)], src, load_sem.at[0])
    load_m = pltpu.make_async_copy(front, tile.at[pl.ds(0, front.shape[0])], load_sem.at[1])
    load_m.start()
    load_src.start()

    raw[core] = jnp.zeros(raw.shape[1:], F32)
    raw[core, :, :shard] = jnp.broadcast_to(impedance[...], (raw.shape[1], shard))

    def lane_block(at_core, k):
        return tile[pl.ds(at_core * lane_blocks + k, rows, stride=2 * lane_blocks)]

    load_m.wait()
    for k in range(lane_blocks):
        m_send[:, k * LANES : (k + 1) * LANES] = lane_block(1 - core, k)
    for k in range(lane_blocks):
        full[core, :, k * LANES : (k + 1) * LANES] = lane_block(core, k)

    @pl.when(layer == 0)
    def _():
        ag_in[...] = jnp.zeros_like(ag_in)

    @pl.when(layer == 0)
    def _():
        pl.semaphore_wait(barrier, cols)

    @pl.when(layer > 0)
    def _():
        pl.semaphore_wait(barrier, cols + half)
        for k in range(half):
            pl.semaphore_signal(
                ready, inc=1, device_id=(layer - 1, (core * half + k) * 2 + core, col), device_id_type=MESH)

    swaps = []
    for k in range(lane_blocks):
        lanes = slice(k * LANES, (k + 1) * LANES)
        swaps.append(pltpu.make_async_remote_copy(
            src_ref=m_send.at[:, lanes], dst_ref=full.at[core, :, lanes], send_sem=swap_send.at[k],
            recv_sem=swap_recv.at[k], device_id=sibling, device_id_type=MESH))
    swaps.append(pltpu.make_async_remote_copy(
        src_ref=raw.at[core], dst_ref=raw.at[core], send_sem=swap_send.at[lane_blocks],
        recv_sem=swap_recv.at[lane_blocks], device_id=sibling, device_id_type=MESH))
    for swap in swaps:
        swap.start()

    load_src.wait()
    for b in range(blocks):
        for k in range(lane_blocks):
            if k < half:
                picked = src[b, pl.ds(2 * shard * k, LANES)]
            else:
                first = 2 * (k - half)
                picked = jnp.concatenate([src[b, pl.ds(2 * shard * i + LANES, HALF)] for i in (first, first + 1)])
            flipped = picked.T
            for c in range(parts_of):
                own[b * parts_of + c, :, k * LANES : (k + 1) * LANES] = flipped[c * WIDE : (c + 1) * WIDE]

    for k in range(lane_blocks):
        swaps[k].wait_recv()
        lanes = slice(k * LANES, (k + 1) * LANES)
        for pair in range(cols // 2):
            first, second = (
                pl.multiple_of(lax.rem(col + d, cols) * shard, 8) for d in ORDER[2 * pair : 2 * pair + 2])
            over = LANES - shard
            picked = [
                jnp.concatenate([full[0, pl.ds(at, shard), lanes], full[1, pl.ds(at, over), lanes]])
                for at in (first, second)
            ]
            picked.append(jnp.concatenate([full[1, pl.ds(at + over, HALF), lanes] for at in (first, second)]))
            for n, values in enumerate(picked):
                flipped = values.T
                high = flipped.astype(BF16)
                low = (flipped - high.astype(F32)).astype(BF16)
                for g in (0, 1):
                    chip, part = divmod(2 * k + g, 3)
                    to = LANES * chip + HALF * part if part < 2 else LANES * half + HALF * chip
                    for i, kept in enumerate((high, low)):
                        at = (3 * i + n) * LANES
                        m_parts[pair, to : to + HALF, at : at + LANES] = kept[g * HALF : (g + 1) * HALF]

    swaps[lane_blocks].wait_recv()
    lane = lax.broadcasted_iota(jnp.int32, raw.shape[1:], 1)
    shifted = turned(raw[1], shard)
    for at in range(0, WIDE, raw.shape[1]):
        scale[at : at + raw.shape[1]] = jnp.where(lane < shard, raw[0], shifted)
    for at in range(WIDE, piece, raw.shape[1]):
        scale[at : at + raw.shape[1]] = left(shifted, turned(shifted, HALF))

    def product(j):
        @pl.when(layer > 0)
        def _():
            pltpu.make_async_copy(ag_in.at[j], ag_in.at[j], ag_recv.at[j]).wait()

        came = [ag_in[j, k, :WIDE] for k in range(half)]
        for k in range(0, half, 2):
            a, b = ag_in[j, k, WIDE:], ag_in[j, k + 1, WIDE:]
            came.append(jnp.concatenate([left(a, turned(b, HALF)), left(turned(a, HALF), b)]))
        total = own[j] + jnp.concatenate(came, axis=1)
        high = total.astype(BF16)
        vec = jnp.concatenate([high, (total - high.astype(F32)).astype(BF16)])
        results = [jnp.dot(vec, m_parts[pair], preferred_element_type=F32) for pair in range(cols // 2)]
        for pair, result in enumerate(results):
            result = result[:WIDE] + result[WIDE:]
            result = result[:, : 3 * LANES] + result[:, 3 * LANES :]
            top, bottom = result[: WIDE // 2, 2 * LANES :], result[WIDE // 2 :, 2 * LANES :]
            rs_out[j, 2 * pair, :WIDE] = result[:, :LANES]
            rs_out[j, 2 * pair, WIDE:] = left(top, turned(bottom, HALF))
            rs_out[j, 2 * pair + 1, :WIDE] = result[:, LANES : 2 * LANES]
            rs_out[j, 2 * pair + 1, WIDE:] = left(turned(top, HALF), bottom)
            for n in (2 * pair, 2 * pair + 1):
                if ORDER[n]:
                    pltpu.make_async_remote_copy(
                        src_ref=rs_out.at[j, n], dst_ref=rs_in.at[j, col * 2 + core], send_sem=rs_send,
                        recv_sem=rs_recv.at[j], device_id=(layer, z * 2 + half_of, lax.rem(col + ORDER[n], cols)),
                        device_id_type=MESH).start()

        @pl.when(jnp.logical_not(is_owner))
        def _():
            pltpu.make_async_remote_copy(
                src_ref=rs_out.at[j, cols - 1], dst_ref=rs_in.at[j, col * 2 + core], send_sem=rs_send,
                recv_sem=rs_recv.at[j], device_id=sibling, device_id_type=MESH).start()

        @pl.when(is_owner)
        def _():
            rs_in[j, col * 2 + core] = rs_out[j, cols - 1]

    def give(b):
        some = ag_out.at[pl.ds(b * parts_of, parts_of)]
        return pltpu.make_async_remote_copy(
            src_ref=some, dst_ref=some, send_sem=out_send.at[b], recv_sem=out_recv.at[b], device_id=sibling,
            device_id_type=MESH)

    def hand_on(j):
        arrived = rs_in.at[j, pl.ds(0, 2 * cols - 1)]
        pltpu.make_async_copy(arrived, arrived, rs_recv.at[j]).wait()
        sums = [rs_in[j, s] for s in range(2 * cols)]
        while len(sums) > 1:
            sums = [x + y for x, y in zip(sums[::2], sums[1::2])]
        total = sums[0]
        ag_out[j] = total * scale[...]

        @pl.when(layer < layers - 1)
        def _():
            @pl.when(j == 0)
            def _():
                pl.semaphore_wait(ready, chips)

            for dz in SPREAD:
                pltpu.make_async_remote_copy(
                    src_ref=ag_out.at[j], dst_ref=ag_in.at[j, z - half_of * half],
                    send_sem=ag_send, recv_sem=ag_recv.at[j],
                    device_id=(layer + 1, lax.rem(z + dz, chips) * 2 + half_of, col), device_id_type=MESH).start()

        @pl.when(lax.rem(j, parts_of) == parts_of - 1)
        def _():
            give(j // parts_of).start()

    def tick(j, _):
        @pl.when(j < chunks)
        def _():
            product(j)

        @pl.when(jnp.logical_and(j >= LAG, is_owner))
        def _():
            hand_on(j - LAG)

        return 0

    lax.fori_loop(0, chunks + LAG, tick, 0)

    for b in range(blocks):
        @pl.when(jnp.logical_not(is_owner))
        def _():
            give(b).wait_recv()

        some = [ag_out[j] for j in range(b * parts_of, (b + 1) * parts_of)]
        first = jnp.concatenate([r[:WIDE] for r in some])
        rest = jnp.concatenate([v for r in some for v in (r[WIDE:], turned(r[WIDE:], HALF))])
        lane = lax.broadcasted_iota(jnp.int32, first.shape, 1)
        over = LANES - shard
        second = jnp.where(lane < over, turned(first, over), turned(rest, over))
        out[b] = jnp.where(core == 0, first, second).T[:shard]

    @pl.when(jnp.logical_not(is_owner))
    def _():
        pltpu.make_async_copy(rs_out, rs_out, rs_send).wait()

    @pl.when(is_owner)
    def _():
        for b in range(blocks):
            give(b).wait_send()
        sent = rs_out.at[:, pl.ds(0, cols - 1)]
        pltpu.make_async_copy(sent, sent, rs_send).wait()

    @pl.when(hands_on)
    def _():
        pltpu.make_async_copy(rs_in, rs_in, ag_send).wait()

    for swap in swaps:
        swap.wait_send()


def solution(mesh):
    layers, chips, cols = mesh.shape["layer"], mesh.shape["row"] // 2, mesh.shape["col"]

    def body(front_inv, impedance, sources):
        rows, depth = front_inv.shape[1], front_inv.shape[3] // 2
        blocks, shard = sources.shape[1], impedance.shape[1]
        chunks, piece = blocks * LANES // WIDE, 2 * shard * WIDE // LANES
        sems = pltpu.SemaphoreType.DMA
        result = pl.pallas_call(
            functools.partial(sweep, (layers, chips, cols)),
            out_shape=jax.ShapeDtypeStruct((blocks, shard, LANES), F32),
            in_specs=[
                pl.BlockSpec(memory_space=pl.ANY),
                pl.BlockSpec(memory_space=pltpu.VMEM),
                pl.BlockSpec(memory_space=pl.ANY),
            ],
            out_specs=pl.BlockSpec(memory_space=pltpu.VMEM),
            scratch_shapes=[
                pltpu.VMEM((rows * 2 * depth // LANES + 16, LANES), F32),
                pltpu.VMEM((rows, depth), F32),
                pltpu.VMEM((2, rows, depth), F32),
                pltpu.VMEM((cols // 2, depth, 2 * rows), BF16),
                pltpu.VMEM((blocks, depth, LANES), F32),
                pltpu.VMEM((chunks, WIDE, depth), F32),
                pltpu.VMEM((chunks, chips // 2, piece, LANES), F32),
                pltpu.VMEM((chunks, cols, piece, LANES), F32),
                pltpu.VMEM((chunks, 2 * cols, piece, LANES), F32),
                pltpu.VMEM((chunks, piece, LANES), F32),
                pltpu.VMEM((2, 8, LANES), F32),
                pltpu.VMEM((piece, LANES), F32),
                pltpu.SemaphoreType.REGULAR,
                sems((2,)),
                sems((depth // LANES + 1,)),
                sems((depth // LANES + 1,)),
                sems,
                sems((chunks,)),
                sems,
                sems((chunks,)),
                sems((blocks,)),
                sems((blocks,)),
            ],
            compiler_params=pltpu.CompilerParams(
                collective_id=0, has_side_effects=True, vmem_limit_bytes=52 * 2**20
            ),
            name="front_sweep",
        )(
            front_inv.reshape(rows * 2 * depth // LANES, LANES),
            impedance,
            sources.reshape(blocks, 2 * depth, LANES),
        )
        return result[None]

    in_specs = (
        P("layer", "row", "col", None),
        P("layer", ("row", "col")),
        P("layer", None, "col", None, None),
    )
    out_specs = P("layer", None, ("row", "col"), None)
    return jax.shard_map(body, mesh=mesh, in_specs=in_specs, out_specs=out_specs, check_vma=False)
```

```python
import functools

import jax
import jax.numpy as jnp
from jax import lax
from jax.experimental import pallas as pl
from jax.experimental.pallas import tpu as pltpu
from jax.sharding import PartitionSpec as P

MESH = pl.DeviceIdType.MESH
F32, BF16 = jnp.float32, jnp.bfloat16
LANES = 128
HALF = LANES // 2
WIDE = 16
LAG = 3
ORDER = (2, 1, 3, 0)
SPREAD = (4, 3, 5, 2, 6, 0, 1, 7)


def left(x, y):
    return jnp.where(lax.broadcasted_iota(jnp.int32, x.shape, 1) < HALF, x, y)


def turned(x, by):
    return pltpu.roll(x, by, 1)


def sweep(sizes, front, impedance, sources, out, tile, m_send, full, m_parts, src, own, ag_in, rs_out, rs_in, ag_out,
          raw, scale, ready, load_sem, swap_send, swap_recv, rs_send, rs_recv, ag_send, ag_recv, out_send, out_recv):
    layers, chips, cols = sizes
    layer, row, col = lax.axis_index("layer"), lax.axis_index("row"), lax.axis_index("col")
    z, core = row // 2, lax.rem(row, 2)
    half = chips // 2
    half_of = z // half
    blocks, shard, _ = out.shape
    parts_of = LANES // WIDE
    chunks = blocks * parts_of
    piece = rs_in.shape[2]
    _, rows, depth = full.shape
    lane_blocks = depth // LANES
    sibling = (layer, z * 2 + 1 - core, col)

    is_owner = core == half_of

    barrier = pltpu.get_barrier_semaphore()

    def greet(device):
        pl.semaphore_signal(barrier, inc=1, device_id=device, device_id_type=MESH)

    hands_on = jnp.logical_and(is_owner, layer < layers - 1)

    @pl.when(hands_on)
    def _():
        for dz in SPREAD:
            greet((layer + 1, lax.rem(z + dz, chips) * 2 + core, col))

    @pl.when(is_owner)
    def _():
        for d in ORDER[:-1]:
            x = lax.rem(col + d, cols)
            greet((layer, z * 2, x))
            greet((layer, z * 2 + 1, x))

    greet(sibling)

    mine = pl.multiple_of(core * depth, LANES)
    load_src = pltpu.make_async_copy(sources.at[:, pl.ds(mine, depth)], src, load_sem.at[0])
    load_m = pltpu.make_async_copy(front, tile.at[pl.ds(0, front.shape[0])], load_sem.at[1])
    load_m.start()
    load_src.start()

    raw[core] = jnp.zeros(raw.shape[1:], F32)
    raw[core, :, :shard] = jnp.broadcast_to(impedance[...], (raw.shape[1], shard))

    def lane_block(at_core, k):
        return tile[pl.ds(at_core * lane_blocks + k, rows, stride=2 * lane_blocks)]

    load_m.wait()
    for k in range(lane_blocks):
        m_send[:, k * LANES : (k + 1) * LANES] = lane_block(1 - core, k)
    for k in range(lane_blocks):
        full[core, :, k * LANES : (k + 1) * LANES] = lane_block(core, k)

    @pl.when(layer == 0)
    def _():
        ag_in[...] = jnp.zeros_like(ag_in)

    @pl.when(layer == 0)
    def _():
        pl.semaphore_wait(barrier, cols)

    @pl.when(layer > 0)
    def _():
        pl.semaphore_wait(barrier, cols + half)
        for k in range(half):
            pl.semaphore_signal(
                ready, inc=1, device_id=(layer - 1, (core * half + k) * 2 + core, col), device_id_type=MESH)

    swaps = []
    for k in range(lane_blocks):
        lanes = slice(k * LANES, (k + 1) * LANES)
        swaps.append(pltpu.make_async_remote_copy(
            src_ref=m_send.at[:, lanes], dst_ref=full.at[core, :, lanes], send_sem=swap_send.at[k],
            recv_sem=swap_recv.at[k], device_id=sibling, device_id_type=MESH))
    swaps.append(pltpu.make_async_remote_copy(
        src_ref=raw.at[core], dst_ref=raw.at[core], send_sem=swap_send.at[lane_blocks],
        recv_sem=swap_recv.at[lane_blocks], device_id=sibling, device_id_type=MESH))
    for swap in swaps:
        swap.start()

    load_src.wait()
    for b in range(blocks):
        for k in range(lane_blocks):
            if k < half:
                picked = src[b, pl.ds(2 * shard * k, LANES)]
            else:
                first = 2 * (k - half)
                picked = jnp.concatenate([src[b, pl.ds(2 * shard * i + LANES, HALF)] for i in (first, first + 1)])
            flipped = picked.T
            for c in range(parts_of):
                own[b * parts_of + c, :, k * LANES : (k + 1) * LANES] = flipped[c * WIDE : (c + 1) * WIDE]

    for k in range(lane_blocks):
        swaps[k].wait_recv()
        lanes = slice(k * LANES, (k + 1) * LANES)
        for pair in range(cols // 2):
            first, second = (
                pl.multiple_of(lax.rem(col + d, cols) * shard, 8) for d in ORDER[2 * pair : 2 * pair + 2])
            over = LANES - shard
            picked = [
                jnp.concatenate([full[0, pl.ds(at, shard), lanes], full[1, pl.ds(at, over), lanes]])
                for at in (first, second)
            ]
            picked.append(jnp.concatenate([full[1, pl.ds(at + over, HALF), lanes] for at in (first, second)]))
            for n, values in enumerate(picked):
                flipped = values.T
                high = flipped.astype(BF16)
                low = (flipped - high.astype(F32)).astype(BF16)
                for g in (0, 1):
                    chip, part = divmod(2 * k + g, 3)
                    to = LANES * chip + HALF * part if part < 2 else LANES * half + HALF * chip
                    for i, kept in enumerate((high, low)):
                        at = (3 * i + n) * LANES
                        m_parts[pair, to : to + HALF, at : at + LANES] = kept[g * HALF : (g + 1) * HALF]

    swaps[lane_blocks].wait_recv()
    lane = lax.broadcasted_iota(jnp.int32, raw.shape[1:], 1)
    shifted = turned(raw[1], shard)
    for at in range(0, WIDE, raw.shape[1]):
        scale[at : at + raw.shape[1]] = jnp.where(lane < shard, raw[0], shifted)
    for at in range(WIDE, piece, raw.shape[1]):
        scale[at : at + raw.shape[1]] = left(shifted, turned(shifted, HALF))

    def product(j):
        @pl.when(layer > 0)
        def _():
            pltpu.make_async_copy(ag_in.at[j], ag_in.at[j], ag_recv.at[j]).wait()

        came = [ag_in[j, k, :WIDE] for k in range(half)]
        for k in range(0, half, 2):
            a, b = ag_in[j, k, WIDE:], ag_in[j, k + 1, WIDE:]
            came.append(jnp.concatenate([left(a, turned(b, HALF)), left(turned(a, HALF), b)]))
        total = own[j] + jnp.concatenate(came, axis=1)
        high = total.astype(BF16)
        vec = jnp.concatenate([high, (total - high.astype(F32)).astype(BF16)])
        results = [jnp.dot(vec, m_parts[pair], preferred_element_type=F32) for pair in range(cols // 2)]
        for pair, result in enumerate(results):
            result = result[:WIDE] + result[WIDE:]
            result = result[:, : 3 * LANES] + result[:, 3 * LANES :]
            top, bottom = result[: WIDE // 2, 2 * LANES :], result[WIDE // 2 :, 2 * LANES :]
            rs_out[j, 2 * pair, :WIDE] = result[:, :LANES]
            rs_out[j, 2 * pair, WIDE:] = left(top, turned(bottom, HALF))
            rs_out[j, 2 * pair + 1, :WIDE] = result[:, LANES : 2 * LANES]
            rs_out[j, 2 * pair + 1, WIDE:] = left(turned(top, HALF), bottom)
            for n in (2 * pair, 2 * pair + 1):
                if ORDER[n]:
                    pltpu.make_async_remote_copy(
                        src_ref=rs_out.at[j, n], dst_ref=rs_in.at[j, col * 2 + core], send_sem=rs_send,
                        recv_sem=rs_recv.at[j], device_id=(layer, z * 2 + half_of, lax.rem(col + ORDER[n], cols)),
                        device_id_type=MESH).start()

        @pl.when(jnp.logical_not(is_owner))
        def _():
            pltpu.make_async_remote_copy(
                src_ref=rs_out.at[j, cols - 1], dst_ref=rs_in.at[j, col * 2 + core], send_sem=rs_send,
                recv_sem=rs_recv.at[j], device_id=sibling, device_id_type=MESH).start()

        @pl.when(is_owner)
        def _():
            rs_in[j, col * 2 + core] = rs_out[j, cols - 1]

    def give(b):
        some = ag_out.at[pl.ds(b * parts_of, parts_of)]
        return pltpu.make_async_remote_copy(
            src_ref=some, dst_ref=some, send_sem=out_send.at[b], recv_sem=out_recv.at[b], device_id=sibling,
            device_id_type=MESH)

    def hand_on(j):
        arrived = rs_in.at[j, pl.ds(0, 2 * cols - 1)]
        pltpu.make_async_copy(arrived, arrived, rs_recv.at[j]).wait()
        sums = [rs_in[j, s] for s in range(2 * cols)]
        while len(sums) > 1:
            sums = [x + y for x, y in zip(sums[::2], sums[1::2])]
        total = sums[0]
        ag_out[j] = total * scale[...]

        @pl.when(layer < layers - 1)
        def _():
            @pl.when(j == 0)
            def _():
                pl.semaphore_wait(ready, chips)

            for dz in SPREAD:
                pltpu.make_async_remote_copy(
                    src_ref=ag_out.at[j], dst_ref=ag_in.at[j, z - half_of * half],
                    send_sem=ag_send, recv_sem=ag_recv.at[j],
                    device_id=(layer + 1, lax.rem(z + dz, chips) * 2 + half_of, col), device_id_type=MESH).start()

        @pl.when(lax.rem(j, parts_of) == parts_of - 1)
        def _():
            give(j // parts_of).start()

    def tick(j, _):
        @pl.when(j < chunks)
        def _():
            product(j)

        @pl.when(jnp.logical_and(j >= LAG, is_owner))
        def _():
            hand_on(j - LAG)

        return 0

    lax.fori_loop(0, chunks + LAG, tick, 0)

    for b in range(blocks):
        @pl.when(jnp.logical_not(is_owner))
        def _():
            give(b).wait_recv()

        some = [ag_out[j] for j in range(b * parts_of, (b + 1) * parts_of)]
        first = jnp.concatenate([r[:WIDE] for r in some])
        rest = jnp.concatenate([v for r in some for v in (r[WIDE:], turned(r[WIDE:], HALF))])
        lane = lax.broadcasted_iota(jnp.int32, first.shape, 1)
        over = LANES - shard
        second = jnp.where(lane < over, turned(first, over), turned(rest, over))
        out[b] = jnp.where(core == 0, first, second).T[:shard]

    @pl.when(jnp.logical_not(is_owner))
    def _():
        pltpu.make_async_copy(rs_out, rs_out, rs_send).wait()

    @pl.when(is_owner)
    def _():
        for b in range(blocks):
            give(b).wait_send()
        sent = rs_out.at[:, pl.ds(0, cols - 1)]
        pltpu.make_async_copy(sent, sent, rs_send).wait()

    @pl.when(hands_on)
    def _():
        pltpu.make_async_copy(rs_in, rs_in, ag_send).wait()

    for swap in swaps:
        swap.wait_send()


def solution(mesh):
    layers, chips, cols = mesh.shape["layer"], mesh.shape["row"] // 2, mesh.shape["col"]

    def body(front_inv, impedance, sources):
        rows, depth = front_inv.shape[1], front_inv.shape[3] // 2
        blocks, shard = sources.shape[1], impedance.shape[1]
        chunks, piece = blocks * LANES // WIDE, 2 * shard * WIDE // LANES
        sems = pltpu.SemaphoreType.DMA
        result = pl.pallas_call(
            functools.partial(sweep, (layers, chips, cols)),
            out_shape=jax.ShapeDtypeStruct((blocks, shard, LANES), F32),
            in_specs=[
                pl.BlockSpec(memory_space=pl.ANY),
                pl.BlockSpec(memory_space=pltpu.VMEM),
                pl.BlockSpec(memory_space=pl.ANY),
            ],
            out_specs=pl.BlockSpec(memory_space=pltpu.VMEM),
            scratch_shapes=[
                pltpu.VMEM((rows * 2 * depth // LANES + 16, LANES), F32),
                pltpu.VMEM((rows, depth), F32),
                pltpu.VMEM((2, rows, depth), F32),
                pltpu.VMEM((cols // 2, depth, 2 * rows), BF16),
                pltpu.VMEM((blocks, depth, LANES), F32),
                pltpu.VMEM((chunks, WIDE, depth), F32),
                pltpu.VMEM((chunks, chips // 2, piece, LANES), F32),
                pltpu.VMEM((chunks, cols, piece, LANES), F32),
                pltpu.VMEM((chunks, 2 * cols, piece, LANES), F32),
                pltpu.VMEM((chunks, piece, LANES), F32),
                pltpu.VMEM((2, 8, LANES), F32),
                pltpu.VMEM((piece, LANES), F32),
                pltpu.SemaphoreType.REGULAR,
                sems((2,)),
                sems((depth // LANES + 1,)),
                sems((depth // LANES + 1,)),
                sems,
                sems((chunks,)),
                sems,
                sems((chunks,)),
                sems((blocks,)),
                sems((blocks,)),
            ],
            compiler_params=pltpu.CompilerParams(
                collective_id=0, has_side_effects=True, vmem_limit_bytes=52 * 2**20
            ),
            name="front_sweep",
        )(
            front_inv.reshape(rows * 2 * depth // LANES, LANES),
            impedance,
            sources.reshape(blocks, 2 * depth, LANES),
        )
        return result[None]

    in_specs = (
        P("layer", "row", "col", None),
        P("layer", ("row", "col")),
        P("layer", None, "col", None, None),
    )
    out_specs = P("layer", None, ("row", "col"), None)
    return jax.shard_map(body, mesh=mesh, in_specs=in_specs, out_specs=out_specs, check_vma=False)
```
